256 devices in a mesh: dp: 64 (over y_hi, z, x), inner: 4 (over y_lo, core).
Axes of the slice: x: 4, y: 4 (y_hi: 2, y_lo: 2; y = y_hi * 2 + y_lo), z: 8, core: 2. Of those that a mesh axis runs over, the one named last changes fastest.
Arguments:
- picture_vectors: bfloat16 [131072, 1152], P(('dp', 'inner')), may hold values from -6 to 6
- caption_vectors: bfloat16 [131072, 1152], P(('dp', 'inner')), may hold values from -6 to 6
- matching_caption_position: int32 [131072], P(('dp', 'inner')), may hold values from 0 to 131071
- score_multiplier: float32 [], replicated, may hold values from 5 to 20
- offset_shift: float32 [], replicated, may hold values from -3 to 1
Outputs:
- picture_derivative: float32 [131072, 1152], P(('dp', 'inner'))
- grad_texts: float32 [131072, 1152], P(('dp', 'inner'))
The draws below stay inside these ranges and needn't reach their ends.
All inputs are finite; a program needn't handle non-finite values.
Results may differ from the reference program's by a relative error of at most 0.0041.
Values may be sent and summed in bfloat16 or wider, within the bound.
No kernel may reach another device: no remote copies, remote signals or barrier semaphores. Data moves between devices by JAX's collectives and lax.ppermute only.
A program may use at most 128 MiB of HBM per device.

```python
import math
import jax
import jax.numpy as jnp
from jax import lax

D = 1152
IMG_DEV = 512
BLOCK = 2048
IMAGES = 131072
TEXTS = 131072
N_DP = 64
N_INNER = 4


def with_ends(array, stream_key, smallest, high):
    index_at = [jax.random.randint(jax.random.fold_in(stream_key, axis), (), 0, length) for axis, length in enumerate(array.shape)]
    longest = array.shape.index(max(array.shape))
    next_to = index_at[:longest] + [(index_at[longest] + 1) % array.shape[longest]] + index_at[longest + 1:]
    return array.at[tuple(index_at)].set(smallest).at[tuple(next_to)].set(high)


def levels(own_key, shape, split, least, top_value):
    loudness = 1.0
    for dim, parts in split:
        draws = jax.random.uniform(jax.random.fold_in(jax.random.fold_in(own_key, 6), dim), (parts,), jnp.float32, least / len(split), top_value / len(split))
        loudness = loudness * jnp.repeat(jnp.exp(draws), shape[dim] // parts).reshape((-1,) + (1,) * (len(shape) - 1 - dim))
    return loudness


def normal_values(key, extent, scale, limit, shards=(), kind=jnp.bfloat16):
    array = jax.random.normal(key, extent, jnp.float32) * scale
    if len(shards) > 0:
        array = levels(key, extent, shards, -0.22, 0.18) * array
    return jnp.clip(array, min=-limit, max=limit).astype(kind)


def setup_inputs(seed: int = 0) -> dict:
    streams_of = jax.random.split(jax.random.key(seed), 6)
    picture_vectors = normal_values(streams_of[0], (IMAGES, D), 1.0, 6.0, ((0, 256),))
    caption_vectors = normal_values(streams_of[1], (TEXTS, D), 1.0, 6.0, ((0, 256),))
    matching_caption_position = with_ends(jax.random.randint(streams_of[2], (IMAGES,), 0, TEXTS), jax.random.fold_in(streams_of[2], 1), 0, TEXTS - 1).astype(jnp.int32)
    score_multiplier = jnp.clip(jnp.exp(jax.random.uniform(streams_of[3], (), jnp.float32, math.log(5.0), math.log(20.0))), 5.0, 20.0)
    offset_shift = jnp.clip(jax.random.uniform(streams_of[4], (), jnp.float32, -3.0, 1.0), -3.0, 1.0)
    return dict(picture_vectors=picture_vectors, caption_vectors=caption_vectors, matching_caption_position=matching_caption_position, score_multiplier=score_multiplier, offset_shift=offset_shift)


def normalize(picture_count):
    values = picture_count.astype(jnp.float32)
    scale = lax.rsqrt(lax.optimization_barrier(jnp.sum(values * values, axis=1, keepdims=True)) + 1e-06)
    return (values * scale).astype(jnp.bfloat16)

def reference(picture_vectors, caption_vectors, matching_caption_position, score_multiplier, offset_shift):
    cycle = N_DP
    group = IMG_DEV * N_INNER
    image_norm = normalize(picture_vectors).reshape(cycle, group, D)
    text_norm = normalize(caption_vectors).reshape(cycle, BLOCK, D)
    pairs = matching_caption_position.reshape(cycle, group)
    previous = jnp.roll(text_norm, 1, axis=0)

    def weights(picture_count, caption_tile, pair, index):
        matched_scores = score_multiplier * lax.dot_general(picture_count, caption_tile, (((1,), (1,)), ((), ())), preferred_element_type=jnp.float32) + offset_shift
        columns = index * BLOCK + jnp.arange(BLOCK, dtype=jnp.int32)
        positive = (pair[:, None] == columns[None, :]).astype(jnp.float32)
        return (jax.nn.sigmoid(matched_scores) - positive).astype(jnp.bfloat16)

    def one_group(items):
        picture_count, resident_caption_tile, former_caption_tile, pair, index = items
        prev_index = (index - 1 + cycle) % cycle
        resident_caption_factor = weights(picture_count, resident_caption_tile, pair, index)
        former_caption_factor = weights(picture_count, former_caption_tile, pair, prev_index)
        picture_derivative_total = score_multiplier * (jnp.dot(resident_caption_factor, resident_caption_tile, preferred_element_type=jnp.float32) + jnp.dot(former_caption_factor, former_caption_tile, preferred_element_type=jnp.float32))
        reduced_axes_spec = (((0,), (0,)), ((), ()))
        resident_captions = score_multiplier * lax.dot_general(resident_caption_factor, picture_count, reduced_axes_spec, preferred_element_type=jnp.float32)
        former_captions = score_multiplier * lax.dot_general(former_caption_factor, picture_count, reduced_axes_spec, preferred_element_type=jnp.float32)
        return (picture_derivative_total, resident_captions, former_captions)
    indices = jnp.arange(cycle, dtype=jnp.int32)
    picture_derivative_total, resident_captions, former_captions = lax.map(one_group, (image_norm, text_norm, previous, pairs, indices))
    grad_texts = resident_captions + jnp.roll(former_captions, -1, axis=0)
    return (picture_derivative_total.reshape(IMAGES, D), grad_texts.reshape(TEXTS, D))
```

```python
import functools

import jax
import jax.numpy as jnp
from jax import lax
from jax.experimental import pallas as pl
from jax.experimental.pallas import tpu as pltpu
from jax.sharding import PartitionSpec as P

AXES = ("dp", "inner")
ROWS = 512
BLOCK = 2048
D = 1152
EXTRA = 16
FORWARD = 2
BACK = 2
FR = ROWS // FORWARD
BR = ROWS // BACK


def routes(dp):
    half = dp // 2

    def crossed(g):
        return 2 if g % half == half - 1 else 0

    every = [(g, i) for g in range(dp) for i in range(4)]
    chip = [(g * 4 + i, g * 4 + (i ^ 2)) for g, i in every]
    core = [(g * 4 + i, g * 4 + (i ^ 1)) for g, i in every]
    ahead = [(g * 4 + i, ((g + 1) % dp) * 4 + (i ^ crossed(g))) for g, i in every]
    behind = [(d, s) for s, d in ahead]
    return chip, core, ahead, behind


def unit_rows(values):
    values = values.astype(jnp.float32)
    scale = lax.rsqrt(jnp.sum(values * values, axis=1, keepdims=True) + 1e-06)
    return (values * scale).astype(jnp.bfloat16)


def norm_body(pos_ref, a_ref, t_ref, *outs):
    pos = pos_ref[...]
    for j in range(FORWARD):
        image, text = outs[j], outs[FORWARD + j]
        here = pl.ds(j * FR, FR)
        image[pl.ds(0, FR)] = unit_rows(a_ref[here])
        text[...] = unit_rows(t_ref[here])
        part = pos[:, j * FR : (j + 1) * FR]
        digits = [part & 63, (part >> 6) & 63, part >> 12]
        rows = lax.broadcasted_iota(jnp.int32, (EXTRA, FR), 0)
        coded = jnp.zeros((EXTRA, FR), jnp.int32)
        for n, digit in enumerate(digits):
            coded = jnp.where(rows == n, jnp.broadcast_to(digit, (EXTRA, FR)), coded)
        image[pl.ds(FR, EXTRA)] = jnp.zeros((EXTRA, D), jnp.bfloat16)
        image[pl.ds(FR, EXTRA), pl.ds(0, FR)] = coded.astype(jnp.float32).astype(jnp.bfloat16)


def norms(pos, a, t):
    image = jax.ShapeDtypeStruct((FR + EXTRA, D), jnp.bfloat16)
    text = jax.ShapeDtypeStruct((FR, D), jnp.bfloat16)
    vmem = pl.BlockSpec(memory_space=pltpu.VMEM)
    outs = pl.pallas_call(
        norm_body,
        out_shape=[image] * FORWARD + [text] * FORWARD,
        in_specs=[vmem] * 3,
        out_specs=[vmem] * (2 * FORWARD),
        compiler_params=pltpu.CompilerParams(vmem_limit_bytes=24 << 20),
        cost_estimate=pl.CostEstimate(flops=4 * ROWS * D, bytes_accessed=8 * ROWS * D, transcendentals=0),
        name="norms",
    )(pos, a, t)
    return list(outs[:FORWARD]), list(outs[FORWARD:])


def positions(ref):
    digits = ref[pl.ds(FR, EXTRA), pl.ds(0, FR)].astype(jnp.float32)
    return digits[0:1] + 64.0 * digits[1:2] + 4096.0 * digits[2:3]


def gram_body(scale_ref, base_ref, *refs, nx, ny, with_sum, x_is_image):
    xs, ys = refs[:nx], refs[nx : nx + ny]
    given = refs[nx + ny] if with_sum else None
    out, weights = refs[nx + ny + with_sum :]
    scale, shift = scale_ref[0], scale_ref[1]
    for i, x_ref in enumerate(xs):
        x = x_ref[pl.ds(0, FR)]
        if x_is_image:
            mine = jnp.transpose(jnp.broadcast_to(positions(x_ref), (128, FR)))
        else:
            mine = (base_ref[i] + lax.broadcasted_iota(jnp.int32, (FR, 128), 0)).astype(jnp.float32)
        for j, y_ref in enumerate(ys):
            y = y_ref[pl.ds(0, FR)]
            dots = lax.dot_general(x, y, (((1,), (1,)), ((), ())), preferred_element_type=jnp.float32)
            logits = scale * dots + shift
            w = 1.0 / (1.0 + jnp.exp(-logits))
            hits = []
            for q in range(FR // 128):
                if x_is_image:
                    first = base_ref[j] + 128 * q
                    other = (first + lax.broadcasted_iota(jnp.int32, (FR, 128), 1)).astype(jnp.float32)
                else:
                    other = positions(y_ref)[:, 128 * q : 128 * (q + 1)]
                hits.append(mine == other)
            w = jnp.where(jnp.concatenate(hits, axis=1), w - 1.0, w)
            weights[pl.ds(i * FR, FR), pl.ds(j * FR, FR)] = w.astype(jnp.bfloat16)
    total = 0.0
    for j, y_ref in enumerate(ys):
        w = weights[:, pl.ds(j * FR, FR)]
        total = total + jnp.dot(w, y_ref[pl.ds(0, FR)], preferred_element_type=jnp.float32)
    total = scale * total
    if with_sum:
        total = total + given[...].astype(jnp.float32)
    out[...] = total.astype(out.dtype)


def gram(scales, bases, xs, ys, given, dtype, x_is_image, name):
    nx, ny = len(xs), len(ys)
    rows = nx * FR
    vmem = pl.BlockSpec(memory_space=pltpu.VMEM)
    smem = pl.BlockSpec(memory_space=pltpu.SMEM)
    extra = [] if given is None else [given]
    return pl.pallas_call(
        functools.partial(gram_body, nx=nx, ny=ny, with_sum=len(extra), x_is_image=x_is_image),
        out_shape=jax.ShapeDtypeStruct((rows, D), dtype),
        in_specs=[smem, smem] + [vmem] * (nx + ny + len(extra)),
        out_specs=vmem,
        scratch_shapes=[pltpu.VMEM((rows, ny * FR), jnp.bfloat16)],
        compiler_params=pltpu.CompilerParams(vmem_limit_bytes=32 << 20),
        cost_estimate=pl.CostEstimate(
            flops=4 * rows * ny * FR * D,
            bytes_accessed=2 * (rows + ny * FR) * D + 4 * rows * D,
            transcendentals=rows * ny * FR,
        ),
        name=name,
    )(scales, bases, *xs, *ys, *extra)


def add_body(mine, *refs):
    out = refs[-1]
    for j, got in enumerate(refs[:-1]):
        here = pl.ds(j * BR, BR)
        out[here] = mine[here] + got[...].astype(jnp.float32)


def shards(picture_vectors, caption_vectors, matching_caption_position, score_multiplier, offset_shift):
    dp = lax.axis_size("dp")
    half = dp // 2
    chip, core, ahead, behind = routes(dp)
    here, inner = lax.axis_index("dp"), lax.axis_index("inner")
    move = lambda blocks, route: [lax.ppermute(b, AXES, route) for b in blocks]

    scales = jnp.stack([score_multiplier, offset_shift])
    own = here * BLOCK + inner * ROWS
    mate = here * BLOCK + (inner ^ 1) * ROWS
    past = (here + dp - 1) % dp
    flip = jnp.where(here % half == 0, 2, 0)
    past_own = past * BLOCK + (inner ^ flip) * ROWS
    past_mate = past * BLOCK + (inner ^ 1 ^ flip) * ROWS
    spread = lambda starts: jnp.stack([s + j * FR for s in starts for j in range(FORWARD)]).astype(jnp.int32)

    image, text = norms(matching_caption_position.reshape(1, ROWS), picture_vectors, caption_vectors)
    image_far = move(image, chip)
    text_past = move(text, ahead)
    image_mate = move(image, core)
    text_mate = move(text, core)
    image_far_mate = move(image_far, core)
    text_past_mate = move(text_past, core)

    texts_near = text + text_mate
    texts_past = text_past + text_past_mate
    images_near = image + image_mate
    images_far = image_far + image_far_mate
    near_bases = spread([own, mate])
    past_bases = spread([past_own, past_mate])
    all_bases = spread([own, mate, past_own, past_mate])
    own_bases = spread([own])
    past_own_bases = spread([past_own])

    f32, bf16 = jnp.float32, jnp.bfloat16
    image_sum = gram(scales, near_bases, image, texts_near, None, f32, True, "image_near")
    text_sum = gram(scales, own_bases, text, images_near, None, f32, False, "text_near")
    far_terms = [
        gram(scales, all_bases, [image_far[j]], texts_near + texts_past, None, bf16, True, f"far_{j}")
        for j in range(BACK)
    ]
    past_terms = [
        gram(scales, past_own_bases[j : j + 1], [text_past[j]], images_near + images_far, None, bf16, False, f"past_{j}")
        for j in range(BACK)
    ]
    far_back = move(far_terms, chip)
    past_back = move(past_terms, behind)
    image_sum = gram(scales, past_bases, image, texts_past, image_sum, f32, True, "image_past")
    text_sum = gram(scales, own_bases, text, images_far, text_sum, f32, False, "text_far")
    picture_derivative = image_sum + jnp.concatenate(far_back, axis=0).astype(f32)
    grad_texts = text_sum + jnp.concatenate(past_back, axis=0).astype(f32)
    return (picture_derivative, grad_texts)


def solution(mesh):
    return jax.shard_map(
        shards,
        mesh=mesh,
        in_specs=(P(AXES, None), P(AXES, None), P(AXES), P(), P()),
        out_specs=(P(AXES, None), P(AXES, None)),
        check_vma=False,
    )
```

```python
import functools

import jax
import jax.numpy as jnp
from jax import lax
from jax.experimental import pallas as pl
from jax.experimental.pallas import tpu as pltpu
from jax.sharding import PartitionSpec as P

AXES = ("dp", "inner")
ROWS = 512
BLOCK = 2048
D = 1152
EXTRA = 16
LOG2E = 1.4426950408889634
FR = ROWS // 2
PIECE = 64
VMEM = pl.BlockSpec(memory_space=pltpu.VMEM)
SMEM = pl.BlockSpec(memory_space=pltpu.SMEM)
HBM = pl.BlockSpec(memory_space=pltpu.HBM)
ANY = pl.BlockSpec(memory_space=pl.ANY)


def routes(dp):
    half = dp // 2

    def crossed(g):
        return 2 if g % half == half - 1 else 0

    every = [(g, i) for g in range(dp) for i in range(4)]
    chip = [(g * 4 + i, g * 4 + (i ^ 2)) for g, i in every]
    core = [(g * 4 + i, g * 4 + (i ^ 1)) for g, i in every]
    ahead = [(g * 4 + i, ((g + 1) % dp) * 4 + (i ^ crossed(g))) for g, i in every]
    behind = [(d, s) for s, d in ahead]
    return chip, core, ahead, behind


def after_body(*refs):
    pass


def after(blocks, earlier):
    return pl.pallas_call(
        after_body,
        out_shape=[jax.ShapeDtypeStruct(b.shape, b.dtype) for b in blocks],
        in_specs=[ANY] * (len(blocks) + len(earlier)),
        out_specs=[ANY] * len(blocks),
        input_output_aliases={k: k for k in range(len(blocks))},
        compiler_params=pltpu.CompilerParams(vmem_limit_bytes=1 << 20),
        cost_estimate=pl.CostEstimate(flops=0, bytes_accessed=0, transcendentals=0),
        name="after",
    )(*blocks, *earlier)


def unit_rows(values):
    values = values.astype(jnp.float32)
    scale = lax.rsqrt(jnp.sum(values * values, axis=1, keepdims=True) + 1e-06)
    return (values * scale).astype(jnp.bfloat16)


def fetch(source, held, sems):
    copies = []
    for at in range(0, ROWS, PIECE):
        copies.append(pltpu.make_async_copy(source.at[pl.ds(at, PIECE)], held.at[pl.ds(at, PIECE)], sems.at[at // PIECE]))
        copies[-1].start()
    return copies


def image_norm_body(pos_ref, a_ref, token, image_0, image_1, held, pos_held, sems, pos_sem):
    pos_copy = pltpu.make_async_copy(pos_ref, pos_held, pos_sem)
    pos_copy.start()
    copies = fetch(a_ref, held, sems)
    pos_copy.wait()
    pos = pos_held[...]
    lines = lax.broadcasted_iota(jnp.int32, (EXTRA, ROWS), 0)
    coded = jnp.zeros((EXTRA, ROWS), jnp.int32)
    for k, digit in enumerate([pos & 63, (pos >> 6) & 63, pos >> 12]):
        coded = jnp.where(lines == k, jnp.broadcast_to(digit, (EXTRA, ROWS)), coded)
    image_0[pl.ds(FR, EXTRA)] = jnp.zeros((EXTRA, D), jnp.bfloat16)
    image_0[pl.ds(FR, EXTRA), pl.ds(0, ROWS)] = coded.astype(jnp.float32).astype(jnp.bfloat16)
    for at, out in zip(range(0, ROWS, FR), (image_0, image_1)):
        for k in range(at // PIECE, (at + FR) // PIECE):
            copies[k].wait()
        out[pl.ds(0, FR)] = unit_rows(held[pl.ds(at, FR)])


def text_norm_body(t_ref, text, held, sems):
    copies = fetch(t_ref, held, sems)
    for at in range(0, ROWS, FR):
        for k in range(at // PIECE, (at + FR) // PIECE):
            copies[k].wait()
        text[pl.ds(at, FR)] = unit_rows(held[pl.ds(at, FR)])


def block(rows, dtype=jnp.bfloat16):
    return pltpu.VMEM((rows, D), dtype)


def params(mib):
    return dict(
        compiler_params=pltpu.CompilerParams(vmem_limit_bytes=mib << 20),
        cost_estimate=pl.CostEstimate(flops=0, bytes_accessed=0, transcendentals=0),
    )


def image_norm(pos, a, earlier):
    hbm = lambda x: pltpu.with_memory_space_constraint(x, pltpu.HBM)
    return pl.pallas_call(
        image_norm_body,
        out_shape=[block(FR + EXTRA), block(FR)],
        in_specs=[HBM, HBM, ANY],
        out_specs=[VMEM, VMEM],
        scratch_shapes=[
            block(ROWS),
            pltpu.VMEM((1, ROWS), jnp.int32),
            pltpu.SemaphoreType.DMA((ROWS // PIECE,)),
            pltpu.SemaphoreType.DMA,
        ],
        name="image_norm",
        **params(16),
    )(hbm(pos), hbm(a), earlier)


def text_norm(t):
    hbm = lambda x: pltpu.with_memory_space_constraint(x, pltpu.HBM)
    return pl.pallas_call(
        text_norm_body,
        out_shape=block(ROWS),
        in_specs=[HBM],
        out_specs=VMEM,
        scratch_shapes=[block(ROWS), pltpu.SemaphoreType.DMA((ROWS // PIECE,))],
        name="text_norm",
        **params(16),
    )(hbm(t))


def rows_of(arrays, pieces):
    loaded = [arrays[a][pl.ds(row, n)] for a, row, n in pieces]
    return loaded[0] if len(loaded) == 1 else jnp.concatenate(loaded, axis=0)


def positions(arrays, place):
    array, row, column = place
    digits = arrays[array][pl.ds(row, EXTRA), pl.ds(column, FR)].astype(jnp.float32)
    return digits[0:1] + 64.0 * digits[1:2] + 4096.0 * digits[2:3]


def gram_rows(scale, shift, base_ref, arrays, xs, ys, given, out, weights, x_is_image):
    slope, level = -LOG2E * scale, -LOG2E * shift
    for i, (xr, xp) in enumerate(xs):
        x = rows_of(arrays, xr)
        if x_is_image:
            mine = jnp.transpose(jnp.broadcast_to(positions(arrays, xp), (128, FR)))
        else:
            mine = (base_ref[xp[0]] + xp[1] + lax.broadcasted_iota(jnp.int32, (FR, 128), 0)).astype(jnp.float32)
        for j, (yr, yp) in enumerate(ys):
            y = rows_of(arrays, yr)
            dots = lax.dot_general(x, y, (((1,), (1,)), ((), ())), preferred_element_type=jnp.float32)
            grown = jnp.exp2(dots * slope + level)
            w = pl.reciprocal(1.0 + grown, approx=True)
            if not x_is_image:
                others = positions(arrays, yp)
            hits = []
            for q in range(FR // 128):
                if x_is_image:
                    first = base_ref[yp[0]] + yp[1] + 128 * q
                    other = (first + lax.broadcasted_iota(jnp.int32, (1, 128), 1)).astype(jnp.float32)
                else:
                    other = others[:, 128 * q : 128 * (q + 1)]
                hits.append(mine == other)
            w = jnp.where(jnp.concatenate(hits, axis=1), w - 1.0, w)
            weights[pl.ds(i * FR, FR), pl.ds(j * FR, FR)] = w.astype(jnp.bfloat16)
    total = 0.0
    for j, (yr, _) in enumerate(ys):
        w = weights[pl.ds(0, len(xs) * FR), pl.ds(j * FR, FR)]
        total = total + jnp.dot(w, rows_of(arrays, yr), preferred_element_type=jnp.float32)
    total = scale * total
    if given is not None:
        total = total + given[0][pl.ds(given[1], len(xs) * FR)]
    out[...] = total.astype(out.dtype)


def gram_body(scale_ref, shift_ref, base_ref, *refs, n, n_given, jobs):
    arrays, given = refs[:n], list(refs[n : n + n_given])
    outs, weights = refs[-1 - len(jobs) : -1], refs[-1]
    for out, (xs, ys, with_sum, x_is_image) in zip(outs, jobs):
        before = (given.pop(0), with_sum[0]) if with_sum else None
        gram_rows(scale_ref[0], shift_ref[0], base_ref, arrays, xs, ys, before, out, weights, x_is_image)


def gram(scalars, jobs, earlier, name, far=False):
    arrays, given, plans, outs = [], [], [], []

    def number(array):
        for k, a in enumerate(arrays):
            if a is array:
                return k
        arrays.append(array)
        return len(arrays) - 1

    def place(part):
        pieces, where = part
        pieces = [(number(a), row, n) for a, row, n in pieces]
        return (pieces, (number(where[0]), *where[1:]) if len(where) == 3 else where)

    for xs, ys, before, dtype, x_is_image in jobs:
        plans.append(([place(p) for p in xs], [place(p) for p in ys], before and before[1:], x_is_image))
        outs.append((pltpu.HBM if far else pltpu.VMEM)((len(xs) * FR, D), dtype))
        if before is not None:
            given.append(before[0])
    rows = max(len(p[0]) for p in plans) * FR
    columns = max(len(p[1]) for p in plans) * FR
    return pl.pallas_call(
        functools.partial(gram_body, n=len(arrays), n_given=len(given), jobs=plans),
        out_shape=outs,
        in_specs=[SMEM] * 3 + [VMEM] * (len(arrays) + len(given)) + [ANY] * len(earlier),
        out_specs=[VMEM] * len(outs),
        scratch_shapes=[pltpu.VMEM((rows, columns), jnp.bfloat16)],
        compiler_params=pltpu.CompilerParams(vmem_limit_bytes=20 << 20),
        cost_estimate=pl.CostEstimate(flops=0, bytes_accessed=0, transcendentals=0),
        name=name,
    )(*scalars, *arrays, *given, *earlier)


def add_body(*refs, start):
    total, got, out, token, held, sems = *refs[:2], *refs[-4:]
    token[...] = jnp.zeros(token.shape, token.dtype)
    copies = []
    for k in range(FR // PIECE):
        rows = pl.ds(k * PIECE, PIECE)
        at = pl.ds(start + k * PIECE, PIECE)
        held[rows] = total[at] + got[rows].astype(jnp.float32)
        copies.append(pltpu.make_async_copy(held.at[rows], out.at[at], sems.at[k]))
        copies[-1].start()
    for copy in copies:
        copy.wait()


def add(total, got, out, start, earlier, name):
    given = [] if out is None else [out]
    return pl.pallas_call(
        functools.partial(add_body, start=start),
        out_shape=[jax.ShapeDtypeStruct((ROWS, D), jnp.float32), jax.ShapeDtypeStruct((8, 128), jnp.float32)],
        in_specs=[VMEM, VMEM] + [HBM] * len(given) + [ANY] * len(earlier),
        out_specs=[HBM, VMEM],
        input_output_aliases={2: 0} if given else {},
        scratch_shapes=[pltpu.VMEM((FR, D), jnp.float32), pltpu.SemaphoreType.DMA((FR // PIECE,))],
        compiler_params=pltpu.CompilerParams(vmem_limit_bytes=16 << 20),
        cost_estimate=pl.CostEstimate(flops=0, bytes_accessed=0, transcendentals=0),
        name=name,
    )(total, got, *given, *earlier)


def shards(picture_vectors, caption_vectors, matching_caption_position, score_multiplier, offset_shift):
    dp = lax.axis_size("dp")
    half = dp // 2
    chip, core, ahead, behind = routes(dp)
    here, inner = lax.axis_index("dp"), lax.axis_index("inner")
    move = lambda block, route: lax.ppermute(block, AXES, route)
    f32, bf16 = jnp.float32, jnp.bfloat16

    past = (here + dp - 1) % dp
    flip = jnp.where(here % half == 0, 2, 0)
    starts = [
        here * BLOCK + inner * ROWS,
        here * BLOCK + (inner ^ 1) * ROWS,
        past * BLOCK + (inner ^ flip) * ROWS,
        past * BLOCK + (inner ^ 1 ^ flip) * ROWS,
    ]
    scalars = (score_multiplier.reshape(1), offset_shift.reshape(1), jnp.stack(starts).astype(jnp.int32))
    pos = matching_caption_position.reshape(1, ROWS)

    run = functools.partial(gram, scalars)
    image_job = lambda xs, ys, given, dtype: (xs, ys, given, dtype, True)
    text_job = lambda xs, ys, given, dtype: (xs, ys, given, dtype, False)
    image_parts = lambda a, b: [([(a, 0, FR)], (a, FR, 0)), ([(b, 0, FR)], (a, FR, FR))]
    text_parts = lambda a, n: [([(a, j * FR, FR)], (n, j * FR)) for j in range(2)]

    text = text_norm(caption_vectors)
    past, text_mate = move(text, ahead), move(text, core)
    image = image_norm(pos, picture_vectors, text)
    far, image_mate = [move(b, chip) for b in image], [move(b, core) for b in image]

    images, texts = image_parts(*image), text_parts(text, 0)
    images_near, texts_near = images + image_parts(*image_mate), texts + text_parts(text_mate, 1)
    image_sum, text_sum = run(
        [image_job(images, texts_near, None, f32), text_job(texts, images_near, None, f32)], [], "near", True
    )
    (far_sum,) = run([image_job(image_parts(*far)[:1], texts_near, None, f32)], [image_sum], "far_near")
    (past,) = after([past], [far_sum])
    past_mate = move(past, core)
    texts_past = text_parts(past, 2)
    texts_there = texts_past + text_parts(past_mate, 3)
    (past_sum,) = run([text_job(texts_past[:1], images_near, None, f32)], [], "past_near")
    far = after(far, [past_sum])
    images_far = image_parts(*far)
    images_there = images_far + image_parts(*[move(b, core) for b in far])
    (far_terms_0,) = run([image_job(images_far[:1], texts_there, (far_sum, 0), bf16)], [past_sum], "far_0")
    far_back_0 = move(far_terms_0, chip)
    (past_terms_0,) = run([text_job(texts_past[:1], images_there, (past_sum, 0), bf16)], [far_terms_0], "past_0")
    past_back_0 = move(past_terms_0, behind)
    (far_terms_1,) = run([image_job(images_far[1:], texts_near + texts_there, None, bf16)], [past_terms_0], "far_1")
    far_back_1 = move(far_terms_1, chip)
    (past_terms_1,) = run([text_job(texts_past[1:], images_near + images_there, None, bf16)], [far_terms_1], "past_1")
    past_back_1 = move(past_terms_1, behind)
    image_sum, text_sum = run(
        [
            image_job(images, texts_there, (image_sum, 0), f32),
            text_job(texts, images_there, (text_sum, 0), f32),
        ],
        [past_terms_1],
        "last",
    )
    out_a, done = add(image_sum, far_back_0, None, 0, [], "image_add_0")
    out_t, done = add(text_sum, past_back_0, None, 0, [done], "text_add_0")
    out_a, done = add(image_sum, far_back_1, out_a, FR, [done], "image_add_1")
    out_t, done = add(text_sum, past_back_1, out_t, FR, [done], "text_add_1")
    return (out_a, out_t)


def solution(mesh):
    return jax.shard_map(
        shards,
        mesh=mesh,
        in_specs=(P(AXES, None), P(AXES, None), P(AXES), P(), P()),
        out_specs=(P(AXES, None), P(AXES, None)),
        check_vma=False,
    )
```

```python
import functools

import jax
import jax.numpy as jnp
from jax import lax
from jax.experimental import pallas as pl
from jax.experimental.pallas import tpu as pltpu
from jax.sharding import PartitionSpec as P

AXES = ("dp", "inner")
ROWS = 512
BLOCK = 2048
D = 1152
EXTRA = 16
LOG2E = 1.4426950408889634
FR = ROWS // 2
PIECE = 64
VMEM = pl.BlockSpec(memory_space=pltpu.VMEM)
SMEM = pl.BlockSpec(memory_space=pltpu.SMEM)
HBM = pl.BlockSpec(memory_space=pltpu.HBM)
ANY = pl.BlockSpec(memory_space=pl.ANY)


def routes(dp):
    half = dp // 2

    def crossed(g):
        return 2 if g % half == half - 1 else 0

    every = [(g, i) for g in range(dp) for i in range(4)]
    chip = [(g * 4 + i, g * 4 + (i ^ 2)) for g, i in every]
    core = [(g * 4 + i, g * 4 + (i ^ 1)) for g, i in every]
    ahead = [(g * 4 + i, ((g + 1) % dp) * 4 + (i ^ crossed(g))) for g, i in every]
    behind = [(d, s) for s, d in ahead]
    return chip, core, ahead, behind


def after_body(*refs):
    pass


def after(blocks, earlier):
    return pl.pallas_call(
        after_body,
        out_shape=[jax.ShapeDtypeStruct(b.shape, b.dtype) for b in blocks],
        in_specs=[ANY] * (len(blocks) + len(earlier)),
        out_specs=[ANY] * len(blocks),
        input_output_aliases={k: k for k in range(len(blocks))},
        compiler_params=pltpu.CompilerParams(vmem_limit_bytes=1 << 20),
        cost_estimate=pl.CostEstimate(flops=0, bytes_accessed=0, transcendentals=0),
        name="after",
    )(*blocks, *earlier)


def unit_rows(values):
    values = values.astype(jnp.float32)
    scale = lax.rsqrt(jnp.sum(values * values, axis=1, keepdims=True) + 1e-06)
    return (values * scale).astype(jnp.bfloat16)


def fetch(source, held, sems):
    copies = []
    for at in range(0, ROWS, PIECE):
        copies.append(pltpu.make_async_copy(source.at[pl.ds(at, PIECE)], held.at[pl.ds(at, PIECE)], sems.at[at // PIECE]))
        copies[-1].start()
    return copies


def image_norm_body(pos_ref, a_ref, token, image_0, image_1, held, pos_held, sems, pos_sem):
    pos_copy = pltpu.make_async_copy(pos_ref, pos_held, pos_sem)
    pos_copy.start()
    copies = fetch(a_ref, held, sems)
    pos_copy.wait()
    pos = pos_held[...]
    lines = lax.broadcasted_iota(jnp.int32, (EXTRA, ROWS), 0)
    coded = jnp.zeros((EXTRA, ROWS), jnp.int32)
    for k, digit in enumerate([pos & 63, (pos >> 6) & 63, pos >> 12]):
        coded = jnp.where(lines == k, jnp.broadcast_to(digit, (EXTRA, ROWS)), coded)
    image_0[pl.ds(FR, EXTRA)] = jnp.zeros((EXTRA, D), jnp.bfloat16)
    image_0[pl.ds(FR, EXTRA), pl.ds(0, ROWS)] = coded.astype(jnp.float32).astype(jnp.bfloat16)
    for at, out in zip(range(0, ROWS, FR), (image_0, image_1)):
        for k in range(at // PIECE, (at + FR) // PIECE):
            copies[k].wait()
        out[pl.ds(0, FR)] = unit_rows(held[pl.ds(at, FR)])


def hbm(x):
    return pltpu.with_memory_space_constraint(x, pltpu.HBM)


def scalar_body(scale_ref, shift_ref, out, dp):
    here, inner = lax.axis_index("dp"), lax.axis_index("inner")
    past = lax.rem(here + dp - 1, dp)
    flip = jnp.where(lax.rem(here, dp // 2) == 0, 2, 0)
    values = [scale_ref[0], shift_ref[0]]
    for block_index, role in ((here, inner), (here, inner ^ 1), (past, inner ^ flip), (past, inner ^ flip ^ 1)):
        values.append((block_index * BLOCK + role * ROWS).astype(jnp.float32))
    lanes = lax.broadcasted_iota(jnp.int32, (8, 128), 1)
    found = jnp.zeros((8, 128), jnp.float32)
    for k, value in enumerate(values):
        found = jnp.where(lanes == k, value, found)
    out[...] = found


def scalar_block(scale, shift):
    return pl.pallas_call(
        functools.partial(scalar_body, dp=lax.axis_size("dp")),
        out_shape=pltpu.VMEM((8, 128), jnp.float32),
        in_specs=[SMEM, SMEM],
        out_specs=VMEM,
        name="scalars",
        **params(1),
    )(scale, shift)


def text_norm_body(t_ref, text, held, sems):
    copies = fetch(t_ref, held, sems)
    for at in range(0, ROWS, FR):
        for k in range(at // PIECE, (at + FR) // PIECE):
            copies[k].wait()
        text[pl.ds(at, FR)] = unit_rows(held[pl.ds(at, FR)])


def block(rows, dtype=jnp.bfloat16):
    return pltpu.VMEM((rows, D), dtype)


def params(mib):
    return dict(
        compiler_params=pltpu.CompilerParams(vmem_limit_bytes=mib << 20),
        cost_estimate=pl.CostEstimate(flops=0, bytes_accessed=0, transcendentals=0),
    )


def image_norm(pos, a, earlier):
    return pl.pallas_call(
        image_norm_body,
        out_shape=[block(FR + EXTRA), block(FR)],
        in_specs=[HBM, HBM, ANY],
        out_specs=[VMEM, VMEM],
        scratch_shapes=[
            block(ROWS),
            pltpu.VMEM((1, ROWS), jnp.int32),
            pltpu.SemaphoreType.DMA((ROWS // PIECE,)),
            pltpu.SemaphoreType.DMA,
        ],
        name="image_norm",
        **params(16),
    )(hbm(pos), hbm(a), earlier)


def text_norm(t):
    return pl.pallas_call(
        text_norm_body,
        out_shape=block(ROWS),
        in_specs=[HBM],
        out_specs=VMEM,
        scratch_shapes=[block(ROWS), pltpu.SemaphoreType.DMA((ROWS // PIECE,))],
        name="text_norm",
        **params(16),
    )(hbm(t))


def rows_of(arrays, pieces):
    loaded = [arrays[a][pl.ds(row, n)] for a, row, n in pieces]
    return loaded[0] if len(loaded) == 1 else jnp.concatenate(loaded, axis=0)


def positions(arrays, place):
    array, row, column = place
    digits = arrays[array][pl.ds(row, EXTRA), pl.ds(column, FR)].astype(jnp.float32)
    return digits[0:1] + 64.0 * digits[1:2] + 4096.0 * digits[2:3]


def gram_rows(scalar, arrays, xs, ys, given, out, weights, x_is_image):
    scale, shift, *bases = scalar
    slope, level = -LOG2E * scale, -LOG2E * shift
    for i, (xr, xp) in enumerate(xs):
        x = rows_of(arrays, xr)
        if x_is_image:
            mine = jnp.transpose(jnp.broadcast_to(positions(arrays, xp), (128, FR)))
        else:
            mine = bases[xp[0]] + (xp[1] + lax.broadcasted_iota(jnp.int32, (FR, 128), 0)).astype(jnp.float32)
        for j, (yr, yp) in enumerate(ys):
            y = rows_of(arrays, yr)
            dots = lax.dot_general(x, y, (((1,), (1,)), ((), ())), preferred_element_type=jnp.float32)
            grown = jnp.exp2(dots * slope + level)
            w = pl.reciprocal(1.0 + grown, approx=True)
            if not x_is_image:
                others = positions(arrays, yp)
            hits = []
            for q in range(FR // 128):
                if x_is_image:
                    columns = yp[1] + 128 * q + lax.broadcasted_iota(jnp.int32, (1, 128), 1)
                    other = bases[yp[0]] + columns.astype(jnp.float32)
                else:
                    other = others[:, 128 * q : 128 * (q + 1)]
                hits.append(mine == other)
            w = jnp.where(jnp.concatenate(hits, axis=1), w - 1.0, w)
            weights[pl.ds(i * FR, FR), pl.ds(j * FR, FR)] = w.astype(jnp.bfloat16)
    total = 0.0
    for j, (yr, _) in enumerate(ys):
        w = weights[pl.ds(0, len(xs) * FR), pl.ds(j * FR, FR)]
        total = total + jnp.dot(w, rows_of(arrays, yr), preferred_element_type=jnp.float32)
    total = scale * total
    if given is not None:
        total = total + given[0][pl.ds(given[1], len(xs) * FR)]
    out[...] = total.astype(out.dtype)


def gram_body(scalar_ref, *refs, n, n_given, jobs, kept):
    arrays = refs[:n]
    scalar = [scalar_ref[0:1, k : k + 1] for k in range(6)]
    given = list(refs[n : n + n_given])
    outs, extras, weights = refs[-1 - len(jobs) - len(kept) : -1 - len(kept)], refs[-1 - len(kept) : -1], refs[-1]
    for k, extra in zip(kept, extras):
        extra[...] = arrays[k][...]
    for out, (xs, ys, with_sum, x_is_image) in zip(outs, jobs):
        before = (given.pop(0), with_sum[0]) if with_sum else None
        gram_rows(scalar, arrays, xs, ys, before, out, weights, x_is_image)


def gram(scalars, jobs, earlier, name, far=False, keep=()):
    arrays, given, plans, outs = [], [], [], []

    def number(array):
        for k, a in enumerate(arrays):
            if a is array:
                return k
        arrays.append(array)
        return len(arrays) - 1

    def place(part):
        pieces, where = part
        pieces = [(number(a), row, n) for a, row, n in pieces]
        return (pieces, (number(where[0]), *where[1:]) if len(where) == 3 else where)

    for xs, ys, before, dtype, x_is_image in jobs:
        plans.append(([place(p) for p in xs], [place(p) for p in ys], before and before[1:], x_is_image))
        outs.append((pltpu.HBM if far else pltpu.VMEM)((len(xs) * FR, D), dtype))
        if before is not None:
            given.append(before[0])
    kept = [number(a) for a in keep]
    rows = max(len(p[0]) for p in plans) * FR
    columns = max(len(p[1]) for p in plans) * FR
    return pl.pallas_call(
        functools.partial(gram_body, n=len(arrays), n_given=len(given), jobs=plans, kept=kept),
        out_shape=outs + [block(a.shape[0]) for a in keep],
        in_specs=[VMEM] * (1 + len(arrays) + len(given)) + [ANY] * len(earlier),
        out_specs=[VMEM] * (len(outs) + len(keep)),
        scratch_shapes=[pltpu.VMEM((rows, columns), jnp.bfloat16)],
        compiler_params=pltpu.CompilerParams(vmem_limit_bytes=20 << 20),
        cost_estimate=pl.CostEstimate(flops=0, bytes_accessed=0, transcendentals=0),
        name=name,
    )(scalars, *arrays, *given, *earlier)


def add_body(*refs, start):
    total, got, out, held, sems = *refs[:2], *refs[-3:]
    copies = []
    for k in range(FR // PIECE):
        rows = pl.ds(k * PIECE, PIECE)
        at = pl.ds(start + k * PIECE, PIECE)
        held[rows] = total[at] + got[rows].astype(jnp.float32)
        copies.append(pltpu.make_async_copy(held.at[rows], out.at[at], sems.at[k]))
        copies[-1].start()
    for copy in copies:
        copy.wait()


def add(total, got, out, start, earlier, name):
    given = [] if out is None else [out]
    return pl.pallas_call(
        functools.partial(add_body, start=start),
        out_shape=jax.ShapeDtypeStruct((ROWS, D), jnp.float32),
        in_specs=[VMEM, VMEM] + [HBM] * (len(given) + len(earlier)),
        out_specs=HBM,
        input_output_aliases={2: 0} if given else {},
        scratch_shapes=[pltpu.VMEM((FR, D), jnp.float32), pltpu.SemaphoreType.DMA((FR // PIECE,))],
        name=name,
        **params(16),
    )(total, got, *[hbm(x) for x in given + earlier])


def shards(picture_vectors, caption_vectors, matching_caption_position, score_multiplier, offset_shift):
    dp = lax.axis_size("dp")
    chip, core, ahead, behind = routes(dp)
    f32, bf16 = jnp.float32, jnp.bfloat16
    move = lambda block, route: lax.ppermute(block, AXES, route)

    scalars = scalar_block(score_multiplier.reshape(1), offset_shift.reshape(1))
    pos = matching_caption_position.reshape(1, ROWS)

    run = functools.partial(gram, scalars)
    image_job = lambda xs, ys, given, dtype: (xs, ys, given, dtype, True)
    text_job = lambda xs, ys, given, dtype: (xs, ys, given, dtype, False)
    image_parts = lambda a, b: [([(a, 0, FR)], (a, FR, 0)), ([(b, 0, FR)], (a, FR, FR))]
    text_parts = lambda a, n: [([(a, j * FR, FR)], (n, j * FR)) for j in range(2)]

    text = text_norm(caption_vectors)
    past, text_mate = move(text, ahead), move(text, core)
    image = list(image_norm(pos, picture_vectors, text))
    far, image_mate = [move(b, chip) for b in image], [move(b, core) for b in image]

    images, texts = image_parts(*image), text_parts(text, 0)
    images_near, texts_near = images + image_parts(*image_mate), texts + text_parts(text_mate, 1)
    image_sum, text_sum = run(
        [image_job(images, texts_near, None, f32), text_job(texts, images_near, None, f32)], [], "near", True
    )
    far_sum, *copies = run(
        [image_job(image_parts(*far)[:1], texts_near, None, f32)], [hbm(image_sum)], "far_near", keep=image + image_mate
    )
    (past,) = after([past], [far_sum])
    past_mate = move(past, core)
    texts_past = text_parts(past, 2)
    texts_there = texts_past + text_parts(past_mate, 3)
    (past_sum,) = run(
        [text_job(texts_past[:1], image_parts(*copies[:2]) + image_parts(*copies[2:]), None, f32)], [], "past_near"
    )
    far = after(far, [past_sum])
    images_far = image_parts(*far)
    images_there = images_far + image_parts(*[move(b, core) for b in far])
    (far_terms_0,) = run([image_job(images_far[:1], texts_there, (far_sum, 0), bf16)], [past_sum], "far_0")
    far_back_0 = move(far_terms_0, chip)
    (past_terms_0,) = run(
        [text_job(texts_past[:1], images_there, (past_sum, 0), bf16)], [far_terms_0], "past_0"
    )
    past_back_0 = move(past_terms_0, behind)
    (far_terms_1,) = run(
        [image_job(images_far[1:], texts_there + texts_near, None, bf16)], [past_terms_0], "far_1"
    )
    far_back_1 = move(far_terms_1, chip)
    (past_terms_1,) = run(
        [text_job(texts_past[1:], images_there + images_near, None, bf16)], [far_terms_1], "past_1"
    )
    past_back_1 = move(past_terms_1, behind)
    image_sum, text_sum = run(
        [
            image_job(images, texts_there, (image_sum, 0), f32),
            text_job(texts, images_there, (text_sum, 0), f32),
        ],
        [past_terms_1],
        "last",
    )
    out_a = add(image_sum, far_back_0, None, 0, [], "image_add_0")
    out_t = add(text_sum, past_back_0, None, 0, [out_a], "text_add_0")
    out_a = add(image_sum, far_back_1, out_a, FR, [out_t], "image_add_1")
    out_t = add(text_sum, past_back_1, out_t, FR, [out_a], "text_add_1")
    return (out_a, out_t)


def solution(mesh):
    return jax.shard_map(
        shards,
        mesh=mesh,
        in_specs=(P(AXES, None), P(AXES, None), P(AXES), P(), P()),
        out_specs=(P(AXES, None), P(AXES, None)),
        check_vma=False,
    )
```

```python
import functools

import jax
import jax.numpy as jnp
from jax import lax
from jax.experimental import pallas as pl
from jax.experimental.pallas import tpu as pltpu
from jax.sharding import PartitionSpec as P

AXES = ("dp", "inner")
ROWS = 512
BLOCK = 2048
D = 1152
EXTRA = 16
LOG2E = 1.4426950408889634
FR = ROWS // 2
PIECE = 64
VMEM = pl.BlockSpec(memory_space=pltpu.VMEM)
SMEM = pl.BlockSpec(memory_space=pltpu.SMEM)
HBM = pl.BlockSpec(memory_space=pltpu.HBM)
ANY = pl.BlockSpec(memory_space=pl.ANY)


def routes(dp):
    half = dp // 2

    def crossed(g):
        return 2 if g % half == half - 1 else 0

    every = [(g, i) for g in range(dp) for i in range(4)]
    chip = [(g * 4 + i, g * 4 + (i ^ 2)) for g, i in every]
    core = [(g * 4 + i, g * 4 + (i ^ 1)) for g, i in every]
    ahead = [(g * 4 + i, ((g + 1) % dp) * 4 + (i ^ crossed(g))) for g, i in every]
    behind = [(d, s) for s, d in ahead]
    return chip, core, ahead, behind


def after_body(*refs):
    pass


def after(blocks, earlier):
    return pl.pallas_call(
        after_body,
        out_shape=[jax.ShapeDtypeStruct(b.shape, b.dtype) for b in blocks],
        in_specs=[ANY] * (len(blocks) + len(earlier)),
        out_specs=[ANY] * len(blocks),
        input_output_aliases={k: k for k in range(len(blocks))},
        compiler_params=pltpu.CompilerParams(vmem_limit_bytes=1 << 20),
        cost_estimate=pl.CostEstimate(flops=0, bytes_accessed=0, transcendentals=0),
        name="after",
    )(*blocks, *earlier)


def unit_rows(values):
    values = values.astype(jnp.float32)
    scale = lax.rsqrt(jnp.sum(values * values, axis=1, keepdims=True) + 1e-06)
    return (values * scale).astype(jnp.bfloat16)


def fetch(source, held, sems):
    copies = []
    for at in range(0, ROWS, PIECE):
        copies.append(pltpu.make_async_copy(source.at[pl.ds(at, PIECE)], held.at[pl.ds(at, PIECE)], sems.at[at // PIECE]))
        copies[-1].start()
    return copies


def image_norm_body(pos_ref, a_ref, token, image_0, image_1, again, held, pos_held, sems, pos_sem):
    pos_copy = pltpu.make_async_copy(pos_ref, pos_held, pos_sem)
    pos_copy.start()
    copies = fetch(a_ref, held, sems)
    pos_copy.wait()
    pos = pos_held[...]
    lines = lax.broadcasted_iota(jnp.int32, (EXTRA, ROWS), 0)
    coded = jnp.zeros((EXTRA, ROWS), jnp.int32)
    for k, digit in enumerate([pos & 63, (pos >> 6) & 63, pos >> 12]):
        coded = jnp.where(lines == k, jnp.broadcast_to(digit, (EXTRA, ROWS)), coded)
    image_0[pl.ds(FR, EXTRA)] = jnp.zeros((EXTRA, D), jnp.bfloat16)
    image_0[pl.ds(FR, EXTRA), pl.ds(0, ROWS)] = coded.astype(jnp.float32).astype(jnp.bfloat16)
    for at, out in zip(range(0, ROWS, FR), (image_0, image_1)):
        for k in range(at // PIECE, (at + FR) // PIECE):
            copies[k].wait()
        values = unit_rows(held[pl.ds(at, FR)])
        out[pl.ds(0, FR)] = values
        if at:
            again[...] = values


def hbm(x):
    return pltpu.with_memory_space_constraint(x, pltpu.HBM)


def scalar_body(scale_ref, shift_ref, out, dp):
    here, inner = lax.axis_index("dp"), lax.axis_index("inner")
    past = lax.rem(here + dp - 1, dp)
    flip = jnp.where(lax.rem(here, dp // 2) == 0, 2, 0)
    values = [scale_ref[0], shift_ref[0]]
    for block_index, role in ((here, inner), (here, inner ^ 1), (past, inner ^ flip), (past, inner ^ flip ^ 1)):
        values.append((block_index * BLOCK + role * ROWS).astype(jnp.float32))
    lanes = lax.broadcasted_iota(jnp.int32, (8, 128), 1)
    found = jnp.zeros((8, 128), jnp.float32)
    for k, value in enumerate(values):
        found = jnp.where(lanes == k, value, found)
    out[...] = found


def scalar_block(scale, shift):
    return pl.pallas_call(
        functools.partial(scalar_body, dp=lax.axis_size("dp")),
        out_shape=pltpu.VMEM((8, 128), jnp.float32),
        in_specs=[SMEM, SMEM],
        out_specs=VMEM,
        name="scalars",
        **params(1),
    )(scale, shift)


def text_norm_body(t_ref, text, held, sems):
    copies = fetch(t_ref, held, sems)
    for at in range(0, ROWS, FR):
        for k in range(at // PIECE, (at + FR) // PIECE):
            copies[k].wait()
        text[pl.ds(at, FR)] = unit_rows(held[pl.ds(at, FR)])


def block(rows, dtype=jnp.bfloat16):
    return pltpu.VMEM((rows, D), dtype)


def params(mib):
    return dict(
        compiler_params=pltpu.CompilerParams(vmem_limit_bytes=mib << 20),
        cost_estimate=pl.CostEstimate(flops=0, bytes_accessed=0, transcendentals=0),
    )


def image_norm(pos, a, earlier):
    return pl.pallas_call(
        image_norm_body,
        out_shape=[block(FR + EXTRA), block(FR), pltpu.HBM((FR, D), jnp.bfloat16)],
        in_specs=[HBM, HBM, ANY],
        out_specs=[VMEM] * 3,
        scratch_shapes=[
            block(ROWS),
            pltpu.VMEM((1, ROWS), jnp.int32),
            pltpu.SemaphoreType.DMA((ROWS // PIECE,)),
            pltpu.SemaphoreType.DMA,
        ],
        name="image_norm",
        **params(16),
    )(hbm(pos), hbm(a), earlier)


def text_norm(t):
    return pl.pallas_call(
        text_norm_body,
        out_shape=block(ROWS),
        in_specs=[HBM],
        out_specs=VMEM,
        scratch_shapes=[block(ROWS), pltpu.SemaphoreType.DMA((ROWS // PIECE,))],
        name="text_norm",
        **params(16),
    )(hbm(t))


def rows_of(arrays, pieces):
    loaded = [arrays[a][pl.ds(row, n)] for a, row, n in pieces]
    return loaded[0] if len(loaded) == 1 else jnp.concatenate(loaded, axis=0)


def positions(arrays, place):
    array, row, column = place
    digits = arrays[array][pl.ds(row, EXTRA), pl.ds(column, FR)].astype(jnp.float32)
    return digits[0:1] + 64.0 * digits[1:2] + 4096.0 * digits[2:3]


def gram_rows(scalar, arrays, xs, ys, given, out, weights, x_is_image):
    scale, shift, *bases = scalar
    slope, level = -LOG2E * scale, -LOG2E * shift
    for i, (xr, xp) in enumerate(xs):
        x = rows_of(arrays, xr)
        if x_is_image:
            mine = jnp.transpose(jnp.broadcast_to(positions(arrays, xp), (128, FR)))
        else:
            mine = bases[xp[0]] + (xp[1] + lax.broadcasted_iota(jnp.int32, (FR, 128), 0)).astype(jnp.float32)
        for j, (yr, yp) in enumerate(ys):
            y = rows_of(arrays, yr)
            dots = lax.dot_general(x, y, (((1,), (1,)), ((), ())), preferred_element_type=jnp.float32)
            grown = jnp.exp2(dots * slope + level)
            w = pl.reciprocal(1.0 + grown, approx=True)
            if not x_is_image:
                others = positions(arrays, yp)
            hits = []
            for q in range(FR // 128):
                if x_is_image:
                    columns = yp[1] + 128 * q + lax.broadcasted_iota(jnp.int32, (1, 128), 1)
                    other = bases[yp[0]] + columns.astype(jnp.float32)
                else:
                    other = others[:, 128 * q : 128 * (q + 1)]
                hits.append(mine == other)
            w = jnp.where(jnp.concatenate(hits, axis=1), w - 1.0, w)
            weights[pl.ds(i * FR, FR), pl.ds(j * FR, FR)] = w.astype(jnp.bfloat16)
    total = 0.0
    for j, (yr, _) in enumerate(ys):
        w = weights[pl.ds(0, len(xs) * FR), pl.ds(j * FR, FR)]
        total = total + jnp.dot(w, rows_of(arrays, yr), preferred_element_type=jnp.float32)
    total = scale * total
    if given is not None:
        total = total + given[0][pl.ds(given[1], len(xs) * FR)]
    out[...] = total.astype(out.dtype)


def gram_body(scalar_ref, *refs, n, n_given, jobs, kept):
    arrays = refs[:n]
    scalar = [scalar_ref[0:1, k : k + 1] for k in range(6)]
    given = list(refs[n : n + n_given])
    outs, extras, weights = refs[-1 - len(jobs) - len(kept) : -1 - len(kept)], refs[-1 - len(kept) : -1], refs[-1]
    for k, extra in zip(kept, extras):
        extra[...] = arrays[k][...]
    for out, (xs, ys, with_sum, x_is_image) in zip(outs, jobs):
        before = (given.pop(0), with_sum[0]) if with_sum else None
        gram_rows(scalar, arrays, xs, ys, before, out, weights, x_is_image)


def gram(scalars, jobs, earlier, name, far=False, keep=()):
    arrays, given, plans, outs = [], [], [], []

    def number(array):
        for k, a in enumerate(arrays):
            if a is array:
                return k
        arrays.append(array)
        return len(arrays) - 1

    def place(part):
        pieces, where = part
        pieces = [(number(a), row, n) for a, row, n in pieces]
        return (pieces, (number(where[0]), *where[1:]) if len(where) == 3 else where)

    for xs, ys, before, dtype, x_is_image in jobs:
        plans.append(([place(p) for p in xs], [place(p) for p in ys], before and before[1:], x_is_image))
        outs.append((pltpu.HBM if far else pltpu.VMEM)((len(xs) * FR, D), dtype))
        if before is not None:
            given.append(before[0])
    kept = [number(a) for a in keep]
    rows = max(len(p[0]) for p in plans) * FR
    columns = max(len(p[1]) for p in plans) * FR
    return pl.pallas_call(
        functools.partial(gram_body, n=len(arrays), n_given=len(given), jobs=plans, kept=kept),
        out_shape=outs + [block(a.shape[0]) for a in keep],
        in_specs=[VMEM] * (1 + len(arrays) + len(given)) + [ANY] * len(earlier),
        out_specs=[VMEM] * (len(outs) + len(keep)),
        scratch_shapes=[pltpu.VMEM((rows, columns), jnp.bfloat16)],
        compiler_params=pltpu.CompilerParams(vmem_limit_bytes=20 << 20),
        cost_estimate=pl.CostEstimate(flops=0, bytes_accessed=0, transcendentals=0),
        name=name,
    )(scalars, *arrays, *given, *earlier)


def add_body(*refs, start):
    total, got, out, held, sems = *refs[:2], *refs[-3:]
    copies = []
    for k in range(FR // PIECE):
        rows = pl.ds(k * PIECE, PIECE)
        at = pl.ds(start + k * PIECE, PIECE)
        held[rows] = total[at] + got[rows].astype(jnp.float32)
        copies.append(pltpu.make_async_copy(held.at[rows], out.at[at], sems.at[k]))
        copies[-1].start()
    for copy in copies:
        copy.wait()


def add(total, got, out, start, earlier, name):
    given = [] if out is None else [out]
    return pl.pallas_call(
        functools.partial(add_body, start=start),
        out_shape=jax.ShapeDtypeStruct((ROWS, D), jnp.float32),
        in_specs=[VMEM, VMEM] + [HBM] * (len(given) + len(earlier)),
        out_specs=HBM,
        input_output_aliases={2: 0} if given else {},
        scratch_shapes=[pltpu.VMEM((FR, D), jnp.float32), pltpu.SemaphoreType.DMA((FR // PIECE,))],
        name=name,
        **params(16),
    )(total, got, *[hbm(x) for x in given + earlier])


def shards(picture_vectors, caption_vectors, matching_caption_position, score_multiplier, offset_shift):
    dp = lax.axis_size("dp")
    chip, core, ahead, behind = routes(dp)
    f32, bf16 = jnp.float32, jnp.bfloat16
    move = lambda block, route: lax.ppermute(block, AXES, route)

    scalars = scalar_block(score_multiplier.reshape(1), offset_shift.reshape(1))
    pos = matching_caption_position.reshape(1, ROWS)

    run = functools.partial(gram, scalars)
    image_job = lambda xs, ys, given, dtype: (xs, ys, given, dtype, True)
    text_job = lambda xs, ys, given, dtype: (xs, ys, given, dtype, False)
    image_parts = lambda a, b: [([(a, 0, FR)], (a, FR, 0)), ([(b, 0, FR)], (a, FR, FR))]
    text_parts = lambda a, n: [([(a, j * FR, FR)], (n, j * FR)) for j in range(2)]

    text = text_norm(caption_vectors)
    past, text_mate = move(text, ahead), move(text, core)
    *image, again = image_norm(pos, picture_vectors, text)
    far, image_mate = [move(image[0], chip)], [move(b, core) for b in image]

    images, texts = image_parts(*image), text_parts(text, 0)
    images_near, texts_near = images + image_parts(*image_mate), texts + text_parts(text_mate, 1)
    (image_sum,) = run([image_job(images, texts_near, None, f32)], [], "near_image", True)
    (again,) = after([again], [hbm(image_sum)])
    far.append(move(again, chip))
    (text_sum,) = run([text_job(texts, images_near, None, f32)], [again], "near_text", True)
    far_sum, *copies = run(
        [image_job(image_parts(*far)[:1], texts_near, None, f32)],
        [hbm(text_sum)],
        "far_near",
        keep=image + image_mate,
    )
    (past,) = after([past], [far_sum])
    past_mate = move(past, core)
    texts_past = text_parts(past, 2)
    texts_there = texts_past + text_parts(past_mate, 3)
    (past_sum,) = run(
        [text_job(texts_past[:1], image_parts(*copies[:2]) + image_parts(*copies[2:]), None, f32)], [], "past_near"
    )
    far = after(far, [past_sum])
    images_far = image_parts(*far)
    images_there = images_far + image_parts(*[move(b, core) for b in far])
    (far_terms_0,) = run([image_job(images_far[:1], texts_there, (far_sum, 0), bf16)], [past_sum], "far_0")
    far_back_0 = move(far_terms_0, chip)
    (past_terms_0,) = run(
        [text_job(texts_past[:1], images_there, (past_sum, 0), bf16)], [far_terms_0], "past_0"
    )
    past_back_0 = move(past_terms_0, behind)
    (far_terms_1,) = run(
        [image_job(images_far[1:], texts_there + texts_near, None, bf16)], [past_terms_0], "far_1"
    )
    far_back_1 = move(far_terms_1, chip)
    (past_terms_1,) = run(
        [text_job(texts_past[1:], images_there + images_near, None, bf16)], [far_terms_1], "past_1"
    )
    past_back_1 = move(past_terms_1, behind)
    image_sum, text_sum = run(
        [
            image_job(images, texts_there, (image_sum, 0), f32),
            text_job(texts, images_there, (text_sum, 0), f32),
        ],
        [past_terms_1],
        "last",
    )
    out_a = add(image_sum, far_back_0, None, 0, [], "image_add_0")
    out_t = add(text_sum, past_back_0, None, 0, [out_a], "text_add_0")
    out_a = add(image_sum, far_back_1, out_a, FR, [out_t], "image_add_1")
    out_t = add(text_sum, past_back_1, out_t, FR, [out_a], "text_add_1")
    return (out_a, out_t)


def solution(mesh):
    return jax.shard_map(
        shards,
        mesh=mesh,
        in_specs=(P(AXES, None), P(AXES, None), P(AXES), P(), P()),
        out_specs=(P(AXES, None), P(AXES, None)),
        check_vma=False,
    )
```

```python
import functools

import jax
import jax.numpy as jnp
from jax import lax
from jax.experimental import pallas as pl
from jax.experimental.pallas import tpu as pltpu
from jax.sharding import PartitionSpec as P

AXES = ("dp", "inner")
ROWS = 512
BLOCK = 2048
D = 1152
EXTRA = 16
LOG2E = 1.4426950408889634
FR = ROWS // 2
PIECE = 64
VMEM = pl.BlockSpec(memory_space=pltpu.VMEM)
SMEM = pl.BlockSpec(memory_space=pltpu.SMEM)
HBM = pl.BlockSpec(memory_space=pltpu.HBM)
ANY = pl.BlockSpec(memory_space=pl.ANY)


def routes(dp):
    half = dp // 2

    def crossed(g):
        return 2 if g % half == half - 1 else 0

    every = [(g, i) for g in range(dp) for i in range(4)]
    chip = [(g * 4 + i, g * 4 + (i ^ 2)) for g, i in every]
    core = [(g * 4 + i, g * 4 + (i ^ 1)) for g, i in every]
    ahead = [(g * 4 + i, ((g + 1) % dp) * 4 + (i ^ crossed(g))) for g, i in every]
    behind = [(d, s) for s, d in ahead]
    return chip, core, ahead, behind


def after_body(*refs):
    pass


def after(blocks, earlier):
    return pl.pallas_call(
        after_body,
        out_shape=[jax.ShapeDtypeStruct(b.shape, b.dtype) for b in blocks],
        in_specs=[ANY] * (len(blocks) + len(earlier)),
        out_specs=[ANY] * len(blocks),
        input_output_aliases={k: k for k in range(len(blocks))},
        compiler_params=pltpu.CompilerParams(vmem_limit_bytes=1 << 20),
        cost_estimate=pl.CostEstimate(flops=0, bytes_accessed=0, transcendentals=0),
        name="after",
    )(*blocks, *earlier)


def unit_rows(values):
    values = values.astype(jnp.float32)
    scale = lax.rsqrt(jnp.sum(values * values, axis=1, keepdims=True) + 1e-06)
    return (values * scale).astype(jnp.bfloat16)


def fetch(source, held, sems):
    copies = []
    for at in range(0, ROWS, PIECE):
        copies.append(pltpu.make_async_copy(source.at[pl.ds(at, PIECE)], held.at[pl.ds(at, PIECE)], sems.at[at // PIECE]))
        copies[-1].start()
    return copies


def image_norm_body(pos_ref, a_ref, token, image_0, image_1, again, held, pos_held, sems, pos_sem):
    pos_copy = pltpu.make_async_copy(pos_ref, pos_held, pos_sem)
    pos_copy.start()
    copies = fetch(a_ref, held, sems)
    pos_copy.wait()
    pos = pos_held[...]
    lines = lax.broadcasted_iota(jnp.int32, (EXTRA, ROWS), 0)
    coded = jnp.zeros((EXTRA, ROWS), jnp.int32)
    for k, digit in enumerate([pos & 63, (pos >> 6) & 63, pos >> 12]):
        coded = jnp.where(lines == k, jnp.broadcast_to(digit, (EXTRA, ROWS)), coded)
    image_0[pl.ds(FR, EXTRA)] = jnp.zeros((EXTRA, D), jnp.bfloat16)
    image_0[pl.ds(FR, EXTRA), pl.ds(0, ROWS)] = coded.astype(jnp.float32).astype(jnp.bfloat16)
    for at, out in zip(range(0, ROWS, FR), (image_0, image_1)):
        for k in range(at // PIECE, (at + FR) // PIECE):
            copies[k].wait()
        values = unit_rows(held[pl.ds(at, FR)])
        out[pl.ds(0, FR)] = values
        if at:
            again[...] = values


def hbm(x):
    return pltpu.with_memory_space_constraint(x, pltpu.HBM)


def scalar_body(scale_ref, shift_ref, out, dp):
    here, inner = lax.axis_index("dp"), lax.axis_index("inner")
    past = lax.rem(here + dp - 1, dp)
    flip = jnp.where(lax.rem(here, dp // 2) == 0, 2, 0)
    values = [scale_ref[0], shift_ref[0]]
    for block_index, role in ((here, inner), (here, inner ^ 1), (past, inner ^ flip), (past, inner ^ flip ^ 1)):
        values.append((block_index * BLOCK + role * ROWS).astype(jnp.float32))
    lanes = lax.broadcasted_iota(jnp.int32, (8, 128), 1)
    found = jnp.zeros((8, 128), jnp.float32)
    for k, value in enumerate(values):
        found = jnp.where(lanes == k, value, found)
    out[...] = found


def scalar_block(scale, shift):
    return pl.pallas_call(
        functools.partial(scalar_body, dp=lax.axis_size("dp")),
        out_shape=pltpu.VMEM((8, 128), jnp.float32),
        in_specs=[SMEM, SMEM],
        out_specs=VMEM,
        name="scalars",
        **params(1),
    )(scale, shift)


def text_norm_body(t_ref, text, held, sems):
    copies = fetch(t_ref, held, sems)
    for at in range(0, ROWS, FR):
        for k in range(at // PIECE, (at + FR) // PIECE):
            copies[k].wait()
        text[pl.ds(at, FR)] = unit_rows(held[pl.ds(at, FR)])


def block(rows, dtype=jnp.bfloat16):
    return pltpu.VMEM((rows, D), dtype)


def params(mib):
    return dict(
        compiler_params=pltpu.CompilerParams(vmem_limit_bytes=mib << 20),
        cost_estimate=pl.CostEstimate(flops=0, bytes_accessed=0, transcendentals=0),
    )


def image_norm(pos, a, earlier):
    return pl.pallas_call(
        image_norm_body,
        out_shape=[block(FR + EXTRA), block(FR), pltpu.HBM((FR, D), jnp.bfloat16)],
        in_specs=[HBM, HBM, ANY],
        out_specs=[VMEM] * 3,
        scratch_shapes=[
            block(ROWS),
            pltpu.VMEM((1, ROWS), jnp.int32),
            pltpu.SemaphoreType.DMA((ROWS // PIECE,)),
            pltpu.SemaphoreType.DMA,
        ],
        name="image_norm",
        **params(16),
    )(hbm(pos), hbm(a), earlier)


def text_norm(t):
    return pl.pallas_call(
        text_norm_body,
        out_shape=block(ROWS),
        in_specs=[HBM],
        out_specs=VMEM,
        scratch_shapes=[block(ROWS), pltpu.SemaphoreType.DMA((ROWS // PIECE,))],
        name="text_norm",
        **params(16),
    )(hbm(t))


def rows_of(arrays, pieces):
    loaded = [arrays[a][pl.ds(row, n)] for a, row, n in pieces]
    return loaded[0] if len(loaded) == 1 else jnp.concatenate(loaded, axis=0)


def positions(arrays, place):
    array, row, column = place
    digits = arrays[array][pl.ds(row, EXTRA), pl.ds(column, FR)].astype(jnp.float32)
    return digits[0:1] + 64.0 * digits[1:2] + 4096.0 * digits[2:3]


def gram_rows(scalar, arrays, xs, ys, given, out, weights, x_is_image):
    scale, shift, *bases = scalar
    slope, level = -LOG2E * scale, -LOG2E * shift
    for i, (xr, xp) in enumerate(xs):
        x = rows_of(arrays, xr)
        if x_is_image:
            mine = jnp.transpose(jnp.broadcast_to(positions(arrays, xp), (128, FR)))
        else:
            mine = bases[xp[0]] + (xp[1] + lax.broadcasted_iota(jnp.int32, (FR, 128), 0)).astype(jnp.float32)
        for j, (yr, yp) in enumerate(ys):
            y = rows_of(arrays, yr)
            dots = lax.dot_general(x, y, (((1,), (1,)), ((), ())), preferred_element_type=jnp.float32)
            grown = jnp.exp2(dots * slope + level)
            w = pl.reciprocal(1.0 + grown, approx=True)
            if not x_is_image:
                others = positions(arrays, yp)
            hits = []
            for q in range(FR // 128):
                if x_is_image:
                    columns = yp[1] + 128 * q + lax.broadcasted_iota(jnp.int32, (1, 128), 1)
                    other = bases[yp[0]] + columns.astype(jnp.float32)
                else:
                    other = others[:, 128 * q : 128 * (q + 1)]
                hits.append(mine == other)
            w = jnp.where(jnp.concatenate(hits, axis=1), w - 1.0, w)
            weights[pl.ds(i * FR, FR), pl.ds(j * FR, FR)] = w.astype(jnp.bfloat16)
    total = 0.0
    for j, (yr, _) in enumerate(ys):
        w = weights[pl.ds(0, len(xs) * FR), pl.ds(j * FR, FR)]
        total = total + jnp.dot(w, rows_of(arrays, yr), preferred_element_type=jnp.float32)
    total = scale * total
    if given is not None:
        total = total + given[0][pl.ds(given[1], len(xs) * FR)]
    rows = total.shape[0] // len(out)
    for k, ref in enumerate(out):
        ref[...] = total[k * rows : (k + 1) * rows].astype(ref.dtype)


def gram_body(scalar_ref, *refs, n, n_given, jobs, kept, halves):
    arrays = refs[:n]
    scalar = [scalar_ref[0:1, k : k + 1] for k in range(6)]
    given = list(refs[n : n + n_given])
    n_outs = halves * len(jobs)
    outs, extras, weights = refs[-1 - n_outs - len(kept) : -1 - len(kept)], refs[-1 - len(kept) : -1], refs[-1]
    outs = [outs[k : k + halves] for k in range(0, n_outs, halves)]
    for k, extra in zip(kept, extras):
        extra[...] = arrays[k][...]
    for out, (xs, ys, with_sum, x_is_image) in zip(outs, jobs):
        before = (given.pop(0), with_sum[0]) if with_sum else None
        gram_rows(scalar, arrays, xs, ys, before, out, weights, x_is_image)


def gram(scalars, jobs, earlier, name, far=False, keep=(), halves=1):
    arrays, given, plans, outs = [], [], [], []

    def number(array):
        for k, a in enumerate(arrays):
            if a is array:
                return k
        arrays.append(array)
        return len(arrays) - 1

    def place(part):
        pieces, where = part
        pieces = [(number(a), row, n) for a, row, n in pieces]
        return (pieces, (number(where[0]), *where[1:]) if len(where) == 3 else where)

    for xs, ys, before, dtype, x_is_image in jobs:
        plans.append(([place(p) for p in xs], [place(p) for p in ys], before and before[1:], x_is_image))
        outs += [(pltpu.HBM if far else pltpu.VMEM)((len(xs) * FR // halves, D), dtype)] * halves
        if before is not None:
            given.append(before[0])
    kept = [number(a) for a in keep]
    rows = max(len(p[0]) for p in plans) * FR
    columns = max(len(p[1]) for p in plans) * FR
    return pl.pallas_call(
        functools.partial(gram_body, n=len(arrays), n_given=len(given), jobs=plans, kept=kept, halves=halves),
        out_shape=outs + [block(a.shape[0]) for a in keep],
        in_specs=[VMEM] * (1 + len(arrays) + len(given)) + [ANY] * len(earlier),
        out_specs=[VMEM] * (len(outs) + len(keep)),
        scratch_shapes=[pltpu.VMEM((rows, columns), jnp.bfloat16)],
        compiler_params=pltpu.CompilerParams(vmem_limit_bytes=20 << 20),
        cost_estimate=pl.CostEstimate(flops=0, bytes_accessed=0, transcendentals=0),
        name=name,
    )(scalars, *arrays, *given, *earlier)


def add_body(*refs, start):
    total, got, out, held, sems = *refs[:2], *refs[-3:]
    copies = []
    for k in range(got.shape[0] // PIECE):
        rows = pl.ds(k * PIECE, PIECE)
        at = pl.ds(start + k * PIECE, PIECE)
        held[rows] = total[at] + got[rows].astype(jnp.float32)
        copies.append(pltpu.make_async_copy(held.at[rows], out.at[at], sems.at[k]))
        copies[-1].start()
    for copy in copies:
        copy.wait()


def add(total, got, out, start, earlier, name):
    given = [] if out is None else [out]
    return pl.pallas_call(
        functools.partial(add_body, start=start),
        out_shape=jax.ShapeDtypeStruct((ROWS, D), jnp.float32),
        in_specs=[VMEM, VMEM] + [HBM] * (len(given) + len(earlier)),
        out_specs=HBM,
        input_output_aliases={2: 0} if given else {},
        scratch_shapes=[pltpu.VMEM(got.shape, jnp.float32), pltpu.SemaphoreType.DMA((got.shape[0] // PIECE,))],
        name=name,
        **params(16),
    )(total, got, *[hbm(x) for x in given + earlier])


def shards(picture_vectors, caption_vectors, matching_caption_position, score_multiplier, offset_shift):
    dp = lax.axis_size("dp")
    chip, core, ahead, behind = routes(dp)
    f32, bf16 = jnp.float32, jnp.bfloat16
    move = lambda block, route: lax.ppermute(block, AXES, route)

    scalars = scalar_block(score_multiplier.reshape(1), offset_shift.reshape(1))
    pos = matching_caption_position.reshape(1, ROWS)

    run = functools.partial(gram, scalars)
    image_job = lambda xs, ys, given, dtype: (xs, ys, given, dtype, True)
    text_job = lambda xs, ys, given, dtype: (xs, ys, given, dtype, False)
    image_parts = lambda a, b: [([(a, 0, FR)], (a, FR, 0)), ([(b, 0, FR)], (a, FR, FR))]
    text_parts = lambda a, n: [([(a, j * FR, FR)], (n, j * FR)) for j in range(2)]

    text = text_norm(caption_vectors)
    past, text_mate = move(text, ahead), move(text, core)
    *image, again = image_norm(pos, picture_vectors, text)
    far, image_mate = [move(image[0], chip)], [move(b, core) for b in image]

    images, texts = image_parts(*image), text_parts(text, 0)
    images_near, texts_near = images + image_parts(*image_mate), texts + text_parts(text_mate, 1)
    (image_sum,) = run([image_job(images, texts_near, None, f32)], [], "near_image", True)
    (again,) = after([again], [hbm(image_sum)])
    far.append(move(again, chip))
    (text_sum,) = run([text_job(texts, images_near, None, f32)], [again], "near_text", True)
    far_sum, *copies = run(
        [image_job(image_parts(*far)[:1], texts_near, None, f32)],
        [hbm(text_sum)],
        "far_near",
        keep=image + image_mate,
    )
    (past,) = after([past], [far_sum])
    past_mate = move(past, core)
    texts_past = text_parts(past, 2)
    texts_there = texts_past + text_parts(past_mate, 3)
    (past_sum,) = run(
        [text_job(texts_past[:1], image_parts(*copies[:2]) + image_parts(*copies[2:]), None, f32)], [], "past_near"
    )
    far = after(far, [past_sum])
    images_far = image_parts(*far)
    images_there = images_far + image_parts(*[move(b, core) for b in far])
    (far_terms_0,) = run([image_job(images_far[:1], texts_there, (far_sum, 0), bf16)], [past_sum], "far_0")
    far_back_0 = move(far_terms_0, chip)
    (past_terms_0,) = run(
        [text_job(texts_past[:1], images_there, (past_sum, 0), bf16)], [far_terms_0], "past_0"
    )
    past_back_0 = move(past_terms_0, behind)
    (far_terms_1,) = run(
        [image_job(images_far[1:], texts_there + texts_near, None, bf16)], [past_terms_0], "far_1"
    )
    far_back_1 = move(far_terms_1, chip)
    past_terms_1, past_terms_2 = run(
        [text_job(texts_past[1:], images_there + images_near, None, bf16)], [far_terms_1], "past_1", halves=2
    )
    past_back_1, past_back_2 = move(past_terms_1, behind), move(past_terms_2, behind)
    image_sum, text_sum = run(
        [
            image_job(images, texts_there, (image_sum, 0), f32),
            text_job(texts, images_there, (text_sum, 0), f32),
        ],
        [past_terms_1],
        "last",
    )
    out_a = add(image_sum, far_back_0, None, 0, [], "image_add_0")
    out_t = add(text_sum, past_back_0, None, 0, [out_a], "text_add_0")
    out_a = add(image_sum, far_back_1, out_a, FR, [out_t], "image_add_1")
    out_t = add(text_sum, past_back_1, out_t, FR, [out_a], "text_add_1")
    out_t = add(text_sum, past_back_2, out_t, FR + FR // 2, [], "text_add_2")
    return (out_a, out_t)


def solution(mesh):
    return jax.shard_map(
        shards,
        mesh=mesh,
        in_specs=(P(AXES, None), P(AXES, None), P(AXES), P(), P()),
        out_specs=(P(AXES, None), P(AXES, None)),
        check_vma=False,
    )
```

```python
import functools

import jax
import jax.numpy as jnp
from jax import lax
from jax.experimental import pallas as pl
from jax.experimental.pallas import tpu as pltpu
from jax.sharding import PartitionSpec as P

AXES = ("dp", "inner")
ROWS = 512
BLOCK = 2048
D = 1152
EXTRA = 16
LOG2E = 1.4426950408889634
FR = ROWS // 2
PIECE = 64
VMEM = pl.BlockSpec(memory_space=pltpu.VMEM)
SMEM = pl.BlockSpec(memory_space=pltpu.SMEM)
HBM = pl.BlockSpec(memory_space=pltpu.HBM)
ANY = pl.BlockSpec(memory_space=pl.ANY)


def routes(dp):
    half = dp // 2

    def crossed(g):
        return 2 if g % half == half - 1 else 0

    every = [(g, i) for g in range(dp) for i in range(4)]
    chip = [(g * 4 + i, g * 4 + (i ^ 2)) for g, i in every]
    core = [(g * 4 + i, g * 4 + (i ^ 1)) for g, i in every]
    ahead = [(g * 4 + i, ((g + 1) % dp) * 4 + (i ^ crossed(g))) for g, i in every]
    behind = [(d, s) for s, d in ahead]
    return chip, core, ahead, behind


def after_body(*refs):
    pass


def after(blocks, earlier):
    return pl.pallas_call(
        after_body,
        out_shape=[jax.ShapeDtypeStruct(b.shape, b.dtype) for b in blocks],
        in_specs=[ANY] * (len(blocks) + len(earlier)),
        out_specs=[ANY] * len(blocks),
        input_output_aliases={k: k for k in range(len(blocks))},
        compiler_params=pltpu.CompilerParams(vmem_limit_bytes=1 << 20),
        cost_estimate=pl.CostEstimate(flops=0, bytes_accessed=0, transcendentals=0),
        name="after",
    )(*blocks, *earlier)


def unit_rows(values):
    values = values.astype(jnp.float32)
    scale = lax.rsqrt(jnp.sum(values * values, axis=1, keepdims=True) + 1e-06)
    return (values * scale).astype(jnp.bfloat16)


def fetch(source, held, sems):
    copies = []
    for at in range(0, ROWS, PIECE):
        copies.append(pltpu.make_async_copy(source.at[pl.ds(at, PIECE)], held.at[pl.ds(at, PIECE)], sems.at[at // PIECE]))
        copies[-1].start()
    return copies


def image_norm_body(pos_ref, a_ref, token, image_0, image_1, again, held, pos_held, sems, pos_sem):
    pos_copy = pltpu.make_async_copy(pos_ref, pos_held, pos_sem)
    pos_copy.start()
    copies = fetch(a_ref, held, sems)
    pos_copy.wait()
    pos = pos_held[...]
    lines = lax.broadcasted_iota(jnp.int32, (EXTRA, ROWS), 0)
    coded = jnp.zeros((EXTRA, ROWS), jnp.int32)
    for k, digit in enumerate([pos & 63, (pos >> 6) & 63, pos >> 12]):
        coded = jnp.where(lines == k, jnp.broadcast_to(digit, (EXTRA, ROWS)), coded)
    image_0[pl.ds(FR, EXTRA)] = jnp.zeros((EXTRA, D), jnp.bfloat16)
    image_0[pl.ds(FR, EXTRA), pl.ds(0, ROWS)] = coded.astype(jnp.float32).astype(jnp.bfloat16)
    for at, out in zip(range(0, ROWS, FR), (image_0, image_1)):
        for k in range(at // PIECE, (at + FR) // PIECE):
            copies[k].wait()
        values = unit_rows(held[pl.ds(at, FR)])
        out[pl.ds(0, FR)] = values
        if at:
            again[...] = values


def hbm(x):
    return pltpu.with_memory_space_constraint(x, pltpu.HBM)


def scalar_body(scale_ref, shift_ref, out, dp):
    here, inner = lax.axis_index("dp"), lax.axis_index("inner")
    past = lax.rem(here + dp - 1, dp)
    flip = jnp.where(lax.rem(here, dp // 2) == 0, 2, 0)
    values = [scale_ref[0], shift_ref[0]]
    for block_index, role in ((here, inner), (here, inner ^ 1), (past, inner ^ flip), (past, inner ^ flip ^ 1)):
        values.append((block_index * BLOCK + role * ROWS).astype(jnp.float32))
    lanes = lax.broadcasted_iota(jnp.int32, (8, 128), 1)
    found = jnp.zeros((8, 128), jnp.float32)
    for k, value in enumerate(values):
        found = jnp.where(lanes == k, value, found)
    out[...] = found


def scalar_block(scale, shift):
    return pl.pallas_call(
        functools.partial(scalar_body, dp=lax.axis_size("dp")),
        out_shape=pltpu.VMEM((8, 128), jnp.float32),
        in_specs=[SMEM, SMEM],
        out_specs=VMEM,
        name="scalars",
        **params(1),
    )(scale, shift)


def text_norm_body(t_ref, text, held, sems):
    copies = fetch(t_ref, held, sems)
    for at in range(0, ROWS, FR):
        for k in range(at // PIECE, (at + FR) // PIECE):
            copies[k].wait()
        text[pl.ds(at, FR)] = unit_rows(held[pl.ds(at, FR)])


def block(rows, dtype=jnp.bfloat16):
    return pltpu.VMEM((rows, D), dtype)


def params(mib):
    return dict(
        compiler_params=pltpu.CompilerParams(vmem_limit_bytes=mib << 20),
        cost_estimate=pl.CostEstimate(flops=0, bytes_accessed=0, transcendentals=0),
    )


def image_norm(pos, a, earlier):
    return pl.pallas_call(
        image_norm_body,
        out_shape=[block(FR + EXTRA), block(FR), pltpu.HBM((FR, D), jnp.bfloat16)],
        in_specs=[HBM, HBM, ANY],
        out_specs=[VMEM] * 3,
        scratch_shapes=[
            block(ROWS),
            pltpu.VMEM((1, ROWS), jnp.int32),
            pltpu.SemaphoreType.DMA((ROWS // PIECE,)),
            pltpu.SemaphoreType.DMA,
        ],
        name="image_norm",
        **params(16),
    )(hbm(pos), hbm(a), earlier)


def text_norm(t):
    return pl.pallas_call(
        text_norm_body,
        out_shape=block(ROWS),
        in_specs=[HBM],
        out_specs=VMEM,
        scratch_shapes=[block(ROWS), pltpu.SemaphoreType.DMA((ROWS // PIECE,))],
        name="text_norm",
        **params(16),
    )(hbm(t))


def rows_of(arrays, pieces):
    loaded = [arrays[a][pl.ds(row, n)] for a, row, n in pieces]
    return loaded[0] if len(loaded) == 1 else jnp.concatenate(loaded, axis=0)


def positions(arrays, place):
    array, row, column = place
    digits = arrays[array][pl.ds(row, EXTRA), pl.ds(column, FR)].astype(jnp.float32)
    return digits[0:1] + 64.0 * digits[1:2] + 4096.0 * digits[2:3]


def gram_rows(scalar, arrays, xs, ys, given, out, weights, x_is_image):
    scale, shift, *bases = scalar
    slope, level = -LOG2E * scale, -LOG2E * shift
    for i, (xr, xp) in enumerate(xs):
        x = rows_of(arrays, xr)
        if x_is_image:
            mine = jnp.transpose(jnp.broadcast_to(positions(arrays, xp), (128, FR)))
        else:
            mine = bases[xp[0]] + (xp[1] + lax.broadcasted_iota(jnp.int32, (FR, 128), 0)).astype(jnp.float32)
        for j, (yr, yp) in enumerate(ys):
            y = rows_of(arrays, yr)
            dots = lax.dot_general(x, y, (((1,), (1,)), ((), ())), preferred_element_type=jnp.float32)
            grown = jnp.exp2(dots * slope + level)
            w = pl.reciprocal(1.0 + grown, approx=True)
            if not x_is_image:
                others = positions(arrays, yp)
            hits = []
            for q in range(FR // 128):
                if x_is_image:
                    columns = yp[1] + 128 * q + lax.broadcasted_iota(jnp.int32, (1, 128), 1)
                    other = bases[yp[0]] + columns.astype(jnp.float32)
                else:
                    other = others[:, 128 * q : 128 * (q + 1)]
                hits.append(mine == other)
            w = jnp.where(jnp.concatenate(hits, axis=1), w - 1.0, w)
            weights[pl.ds(i * FR, FR), pl.ds(j * FR, FR)] = w.astype(jnp.bfloat16)
    total = 0.0
    for j, (yr, _) in enumerate(ys):
        w = weights[pl.ds(0, len(xs) * FR), pl.ds(j * FR, FR)]
        total = total + jnp.dot(w, rows_of(arrays, yr), preferred_element_type=jnp.float32)
    total = scale * total
    if given is not None:
        total = total + given[0][pl.ds(given[1], len(xs) * FR)]
    out[...] = total.astype(out.dtype)


def gram_body(scalar_ref, *refs, n, n_given, jobs, kept):
    arrays = refs[:n]
    scalar = [scalar_ref[0:1, k : k + 1] for k in range(6)]
    given = list(refs[n : n + n_given])
    outs, extras, weights = refs[-1 - len(jobs) - len(kept) : -1 - len(kept)], refs[-1 - len(kept) : -1], refs[-1]
    for k, extra in zip(kept, extras):
        extra[...] = arrays[k][...]
    for out, (xs, ys, with_sum, x_is_image) in zip(outs, jobs):
        before = (given.pop(0), with_sum[0]) if with_sum else None
        gram_rows(scalar, arrays, xs, ys, before, out, weights, x_is_image)


def gram(scalars, jobs, earlier, name, far=False, keep=()):
    arrays, given, plans, outs = [], [], [], []

    def number(array):
        for k, a in enumerate(arrays):
            if a is array:
                return k
        arrays.append(array)
        return len(arrays) - 1

    def place(part):
        pieces, where = part
        pieces = [(number(a), row, n) for a, row, n in pieces]
        return (pieces, (number(where[0]), *where[1:]) if len(where) == 3 else where)

    for xs, ys, before, dtype, x_is_image in jobs:
        plans.append(([place(p) for p in xs], [place(p) for p in ys], before and before[1:], x_is_image))
        outs.append((pltpu.HBM if far else pltpu.VMEM)((len(xs) * FR, D), dtype))
        if before is not None:
            given.append(before[0])
    kept = [number(a) for a in keep]
    rows = max(len(p[0]) for p in plans) * FR
    columns = max(len(p[1]) for p in plans) * FR
    return pl.pallas_call(
        functools.partial(gram_body, n=len(arrays), n_given=len(given), jobs=plans, kept=kept),
        out_shape=outs + [block(a.shape[0]) for a in keep],
        in_specs=[VMEM] * (1 + len(arrays) + len(given)) + [ANY] * len(earlier),
        out_specs=[VMEM] * (len(outs) + len(keep)),
        scratch_shapes=[pltpu.VMEM((rows, columns), jnp.bfloat16)],
        compiler_params=pltpu.CompilerParams(vmem_limit_bytes=20 << 20),
        cost_estimate=pl.CostEstimate(flops=0, bytes_accessed=0, transcendentals=0),
        name=name,
    )(scalars, *arrays, *given, *earlier)


def add_body(*refs, start):
    total, got, out, held, sems = *refs[:2], *refs[-3:]
    copies = []
    for k in range(FR // PIECE):
        rows = pl.ds(k * PIECE, PIECE)
        at = pl.ds(start + k * PIECE, PIECE)
        held[rows] = total[at] + got[rows].astype(jnp.float32)
        copies.append(pltpu.make_async_copy(held.at[rows], out.at[at], sems.at[k]))
        copies[-1].start()
    for copy in copies:
        copy.wait()


def add(total, got, out, start, earlier, name):
    given = [] if out is None else [out]
    return pl.pallas_call(
        functools.partial(add_body, start=start),
        out_shape=jax.ShapeDtypeStruct((ROWS, D), jnp.float32),
        in_specs=[VMEM, VMEM] + [HBM] * (len(given) + len(earlier)),
        out_specs=HBM,
        input_output_aliases={2: 0} if given else {},
        scratch_shapes=[pltpu.VMEM((FR, D), jnp.float32), pltpu.SemaphoreType.DMA((FR // PIECE,))],
        name=name,
        **params(16),
    )(total, got, *[hbm(x) for x in given + earlier])


def shards(picture_vectors, caption_vectors, matching_caption_position, score_multiplier, offset_shift):
    dp = lax.axis_size("dp")
    chip, core, ahead, behind = routes(dp)
    f32, bf16 = jnp.float32, jnp.bfloat16
    move = lambda block, route: lax.ppermute(block, AXES, route)

    scalars = scalar_block(score_multiplier.reshape(1), offset_shift.reshape(1))
    pos = matching_caption_position.reshape(1, ROWS)

    run = functools.partial(gram, scalars)
    image_job = lambda xs, ys, given, dtype: (xs, ys, given, dtype, True)
    text_job = lambda xs, ys, given, dtype: (xs, ys, given, dtype, False)
    image_parts = lambda a, b: [([(a, 0, FR)], (a, FR, 0)), ([(b, 0, FR)], (a, FR, FR))]
    text_parts = lambda a, n: [([(a, j * FR, FR)], (n, j * FR)) for j in range(2)]

    text = text_norm(caption_vectors)
    past, text_mate = move(text, ahead), move(text, core)
    *image, again = image_norm(pos, picture_vectors, text)
    far, image_mate = [move(image[0], chip)], [move(b, core) for b in image]

    images, texts = image_parts(*image), text_parts(text, 0)
    images_near, texts_near = images + image_parts(*image_mate), texts + text_parts(text_mate, 1)
    (image_sum,) = run([image_job(images, texts_near, None, f32)], [], "near_image", True)
    (again,) = after([again], [hbm(image_sum)])
    far.append(move(again, chip))
    (text_sum,) = run([text_job(texts, images_near, None, f32)], [again], "near_text", True)
    far_sum, *copies = run(
        [image_job(image_parts(*far)[:1], texts_near, None, f32)],
        [hbm(text_sum)],
        "far_near",
        keep=image + image_mate,
    )
    (past,) = after([past], [far_sum])
    past_mate = move(past, core)
    texts_past = text_parts(past, 2)
    texts_there = texts_past + text_parts(past_mate, 3)
    far = after(far, [past])
    images_far = image_parts(*far)
    images_there = images_far + image_parts(*[move(b, core) for b in far])
    (past_sum,) = run(
        [text_job(texts_past[:1], image_parts(*copies[:2]) + image_parts(*copies[2:]), None, f32)], far[:1], "past_near"
    )
    (far_terms_0,) = run([image_job(images_far[:1], texts_there, (far_sum, 0), bf16)], [past_sum], "far_0")
    far_back_0 = move(far_terms_0, chip)
    (past_terms_0,) = run(
        [text_job(texts_past[:1], images_there, (past_sum, 0), bf16)], [far_terms_0], "past_0"
    )
    past_back_0 = move(past_terms_0, behind)
    (far_terms_1,) = run(
        [image_job(images_far[1:], texts_there + texts_near, None, bf16)], [past_terms_0], "far_1"
    )
    far_back_1 = move(far_terms_1, chip)
    (past_terms_1,) = run(
        [text_job(texts_past[1:], images_there + images_near, None, bf16)], [far_terms_1], "past_1"
    )
    past_back_1 = move(past_terms_1, behind)
    image_sum, text_sum = run(
        [
            image_job(images, texts_there, (image_sum, 0), f32),
            text_job(texts, images_there, (text_sum, 0), f32),
        ],
        [past_terms_1],
        "last",
    )
    out_a = add(image_sum, far_back_0, None, 0, [], "image_add_0")
    out_t = add(text_sum, past_back_0, None, 0, [out_a], "text_add_0")
    out_a = add(image_sum, far_back_1, out_a, FR, [out_t], "image_add_1")
    out_t = add(text_sum, past_back_1, out_t, FR, [out_a], "text_add_1")
    return (out_a, out_t)


def solution(mesh):
    return jax.shard_map(
        shards,
        mesh=mesh,
        in_specs=(P(AXES, None), P(AXES, None), P(AXES), P(), P()),
        out_specs=(P(AXES, None), P(AXES, None)),
        check_vma=False,
    )
```
